128 devices in a mesh: dom: 128 (over z, y, x, core).
Axes of the slice: x: 4, y: 4, z: 4, core: 2. Of those that a mesh axis runs over, the one named last changes fastest.
Arguments:
- particles: float32 [4, 65536, 128], P(None, 'dom')
- velocities: float32 [3, 6144, 128], P(None, 'dom'), may hold values from -6 to 6
- active_cells: int32 [6144], P('dom'), may hold values from 0 to 511, as said below
- active_counts: int32 [6144], P('dom'), may hold values from 1 to 128
- local_targets: int32 [16384], P('dom'), may hold values from 0 to 47
- local_sources: int32 [16384], P('dom'), may hold values from 0 to 511
- export_lists: int32 [2048, 40], P('dom'), may hold values from 0 to 48, as said below
- remote_slots: int32 [49152], P('dom'), may hold values from 0 to 639, as said below
- remote_cells: int32 [49152], P('dom'), may hold values from -1 to 511, as said below
Outputs:
- kicked: float32 [3, 6144, 128], P(None, 'dom')
- potential: float32 [6144, 128], P('dom')
The draws below stay inside these ranges and needn't reach their ends.
Inputs may be any that keep to these rules, and one draw needn't show every extreme that they name: `export_lists`: each row holds distinct active cells in its used slots, which come first and are followed by 48. At most 40 slots are used; round 0 of every domain whose index is a multiple of 4 uses all 40. Rows for an offset that leaves the curve hold only 48. `remote_slots`: A used pair slot of domain e names slot r * 40 + s of a used export slot s of domain e - off(r) in round r. `remote_cells`: in each domain the used pair slots come first; domain 128 // 2 uses all 384. `active_cells`: each domain's 48 entries are distinct.
All inputs are finite; a program needn't handle non-finite values.
Results may differ from the reference program's by a relative error of at most 0.0003.
Values sent between devices are 32-bit elements; how exact they have to be, the bound alone decides.
A program may use at most 64 MiB of HBM per device.

```python
import math
import jax
import jax.numpy as jnp
from jax import lax

PART = 128
CELLS = 512
ACT = 48
EXP = 40
LP = 128
RP = 384
HOPS = 8
ROUNDS = 16
CELLS_ALL = 65536
ACT_ALL = 6144
N_DOM = 128


def hop_offsets():
    rounds_idx = jnp.arange(ROUNDS, dtype=jnp.int32)
    return jnp.where(rounds_idx < HOPS, rounds_idx + 1, -(rounds_idx - HOPS + 1))


def export_counts(key):
    key = jax.random.fold_in(key, 101)
    counts = jax.random.randint(key, (N_DOM, ROUNDS), 1, EXP + 1)
    device = jnp.arange(N_DOM, dtype=jnp.int32)[:, None]
    rounds_idx = jnp.arange(ROUNDS, dtype=jnp.int32)[None, :]
    counts = jnp.where((device % 4 == 0) & (rounds_idx == 0), EXP, counts)
    dest = device + hop_offsets()[None, :]
    return jnp.where((dest >= 0) & (dest < N_DOM), counts, 0)


def remote_pairs(key):
    counts = export_counts(key)
    key = jax.random.fold_in(key, 103)
    key_round, key_slot, key_cell, key_live = jax.random.split(key, 4)
    device = jnp.arange(N_DOM, dtype=jnp.int32)[:, None]
    hops = hop_offsets()
    chosen = jax.random.randint(key_round, (N_DOM, RP), 0, ROUNDS)
    source = device - hops[chosen]
    outside = (source < 0) | (source >= N_DOM)
    chosen = jnp.where(outside, (chosen + HOPS) % ROUNDS, chosen)
    source = device - hops[chosen]
    avail = counts[source, chosen]
    slot = jax.random.randint(key_slot, (N_DOM, RP), 0, 1048576) % avail
    slots = chosen * EXP + slot
    cells = jax.random.randint(key_cell, (N_DOM, RP), 0, CELLS)
    live_count = jax.random.randint(key_live, (N_DOM,), max(RP // 8, 1), RP + 1)
    live_count = jnp.where(jnp.arange(N_DOM) == N_DOM // 2, RP, live_count)
    live = jnp.arange(RP)[None, :] < live_count[:, None]
    cells = jnp.where(live, cells, -1)
    return (slots.reshape(-1).astype(jnp.int32), cells.reshape(-1).astype(jnp.int32))


def draw_particles(key, part):
    key = jax.random.fold_in(key, 5)
    key_pos, key_mass, key_dom, key_factor = jax.random.split(key, 4)
    positions = jax.random.uniform(key_pos, (3, CELLS_ALL, 128), jnp.float32, 0.0, 2.0)
    masses = jax.random.uniform(key_mass, (1, CELLS_ALL, 128), jnp.float32, 0.5, 1.5)
    heavy_domain = jax.random.randint(key_dom, (), 0, N_DOM)
    factor = jnp.exp(jax.random.uniform(key_factor, (), jnp.float32, jnp.log(3.0), jnp.log(30.0)))
    cell_domain = jnp.arange(CELLS_ALL, dtype=jnp.int32) // CELLS
    boost = jnp.where(cell_domain == heavy_domain, factor, 1.0).astype(jnp.float32)
    masses = masses * boost[None, :, None]
    return jnp.concatenate([positions, masses], axis=0)


def draw_active_cells(key, part):
    key = jax.random.fold_in(key, 4)
    keys = jax.random.split(key, N_DOM)
    picked = jax.vmap(lambda single: jax.random.permutation(single, CELLS)[:ACT])(keys)
    return picked.reshape(-1).astype(jnp.int32)


def draw_export_lists(key, part):
    counts = export_counts(key)
    key = jax.random.fold_in(key, 2)
    keys = jax.random.split(key, N_DOM * ROUNDS)
    picked = jax.vmap(lambda single: jax.random.permutation(single, ACT)[:EXP])(keys).reshape(N_DOM, ROUNDS, EXP)
    slot = jnp.arange(EXP, dtype=jnp.int32)
    lists = jnp.where(slot[None, None, :] < counts[:, :, None], picked, ACT)
    return lists.reshape(N_DOM * ROUNDS, EXP).astype(jnp.int32)


def draw_remote_slots(key, part):
    slots, cells = remote_pairs(key)
    return slots


def draw_remote_cells(key, part):
    slots, cells = remote_pairs(key)
    return cells


def plant(drawn, key, smallest, high):
    place = [jax.random.randint(jax.random.fold_in(key, axis), (), 0, length) for axis, length in enumerate(drawn.shape)]
    main_axis = drawn.shape.index(max(drawn.shape))
    neighbour = place[:main_axis] + [(place[main_axis] + 1) % drawn.shape[main_axis]] + place[main_axis + 1:]
    return drawn.at[tuple(place)].set(smallest).at[tuple(neighbour)].set(high)


def shard_levels(stream_key, shape, pieces, low, largest):
    factor_of = 1.0
    for dim, shards_of in pieces:
        steps = jax.random.uniform(jax.random.fold_in(jax.random.fold_in(stream_key, 6), dim), (shards_of,), jnp.float32, low / len(pieces), largest / len(pieces))
        factor_of = factor_of * jnp.repeat(jnp.exp(steps), shape[dim] // shards_of).reshape((-1,) + (1,) * (len(shape) - 1 - dim))
    return factor_of


def noise(stream_key, dims, scale, bound, shards=(), kind=jnp.bfloat16):
    gain = shard_levels(stream_key, dims, shards, -0.22, 0.18) if shards else 1.0
    values = jax.random.normal(stream_key, dims, jnp.float32) * scale * gain
    return jnp.minimum(jnp.maximum(values, -bound), bound).astype(kind)


def setup_inputs(seed: int = 0) -> dict:
    key_of = jax.random.split(jax.random.key(seed), 10)
    particles = draw_particles(jax.random.fold_in(key_of[9], 71), 0)
    velocities = noise(key_of[1], (3, ACT_ALL, PART), 1.0, 6.0, ((1, 128),), jnp.float32)
    active_cells = draw_active_cells(jax.random.fold_in(key_of[9], 71), 0)
    active_counts = plant(jax.random.randint(key_of[3], (ACT_ALL,), 1, 129), jax.random.fold_in(key_of[3], 1), 1, 128).astype(jnp.int32)
    local_targets = plant(jax.random.randint(key_of[4], (LP * N_DOM,), 0, ACT), jax.random.fold_in(key_of[4], 1), 0, ACT - 1).astype(jnp.int32)
    local_sources = plant(jax.random.randint(key_of[5], (LP * N_DOM,), 0, CELLS), jax.random.fold_in(key_of[5], 1), 0, CELLS - 1).astype(jnp.int32)
    export_lists = draw_export_lists(jax.random.fold_in(key_of[9], 71), 0)
    remote_slots = draw_remote_slots(jax.random.fold_in(key_of[9], 71), 0)
    remote_cells = draw_remote_cells(jax.random.fold_in(key_of[9], 71), 0)
    return dict(particles=particles, velocities=velocities, active_cells=active_cells, active_counts=active_counts, local_targets=local_targets, local_sources=local_sources, export_lists=export_lists, remote_slots=remote_slots, remote_cells=remote_cells)


soften_sq = 0.0025
split_inv = 1.0
split_coef = 1.1283791670955126
grav_const = 0.001
step_max = 1.0
accel_ref = 0.1

def pair_terms(targets, sources):
    delta = sources[:3, :, None, :] - targets[:, :, :, None]
    dist_sq = lax.optimization_barrier(jnp.sum(delta * delta, axis=0)) + soften_sq
    dist = jnp.sqrt(dist_sq)
    tail = jax.scipy.special.erfc(dist * split_inv)
    kernel = tail + dist * split_coef * jnp.exp(-dist_sq * split_inv * split_inv)
    masses = sources[3][:, None, :]
    weight = masses * kernel / (dist_sq * dist)
    accel = grav_const * lax.optimization_barrier(jnp.sum(delta * weight[None], axis=-1))
    pot = -grav_const * lax.optimization_barrier(jnp.sum(masses * tail / dist, axis=-1))
    return jnp.concatenate([accel, pot[None]], axis=0)

def blocked_terms(targets, sources):
    count = targets.shape[1]
    block = math.gcd(64, count)
    target_blocks = jnp.moveaxis(targets.reshape(3, count // block, block, 128), 1, 0)
    source_blocks = jnp.moveaxis(sources.reshape(4, count // block, block, 128), 1, 0)
    terms = lax.map(lambda pair: pair_terms(pair[0], pair[1]), (target_blocks, source_blocks))
    return jnp.moveaxis(terms, 0, 1).reshape(4, count, 128)

def offsets_list(half):
    return [k + 1 for k in range(half)] + [-(k + 1) for k in range(half)]

def reference(particles, velocities, active_cells, active_counts, local_targets, local_sources, export_lists, remote_slots, remote_cells):
    shifts = jnp.array(offsets_list(HOPS), jnp.int32)
    rounds_idx = jnp.arange(ROUNDS, dtype=jnp.int32)
    act_cells = active_cells.reshape(N_DOM, ACT)
    exports = export_lists.reshape(N_DOM, ROUNDS, EXP)
    loc_t = local_targets.reshape(N_DOM, LP)
    loc_s = local_sources.reshape(N_DOM, LP)
    rem_k = remote_slots.reshape(N_DOM, RP)
    rem_c = remote_cells.reshape(N_DOM, RP)
    act_rows = jnp.arange(ACT, dtype=jnp.int32)
    slot_rows = jnp.arange(ROUNDS * EXP, dtype=jnp.int32)

    def own_targets(dev):
        return jnp.take(particles[:3], act_cells[dev] + dev * CELLS, axis=1)

    def sending(dev):
        flat = exports[dev].reshape(-1)
        used = (flat < ACT).astype(jnp.float32)
        picked = jnp.take(own_targets(dev), jnp.minimum(flat, ACT - 1), axis=1)
        return picked * used[None, :, None]
    sent = lax.map(sending, jnp.arange(N_DOM, dtype=jnp.int32)).reshape(N_DOM, 3, ROUNDS, EXP, 128)

    def device_forces(dev):
        src = dev - shifts
        valid = ((src >= 0) & (src < N_DOM)).astype(jnp.float32)
        recv = sent[jnp.clip(src, 0, N_DOM - 1), :, rounds_idx] * valid[:, None, None, None]
        recv = jnp.moveaxis(recv, 0, 1).reshape(3, ROUNDS * EXP, 128)
        targets = jnp.concatenate([jnp.take(own_targets(dev), loc_t[dev], axis=1), jnp.take(recv, rem_k[dev], axis=1)], axis=1)
        sources = jnp.concatenate([jnp.take(particles, loc_s[dev] + dev * CELLS, axis=1), jnp.take(particles, jnp.maximum(rem_c[dev], 0) + dev * CELLS, axis=1)], axis=1)
        terms = blocked_terms(targets, sources)
        local_hot = (loc_t[dev][None, :] == act_rows[:, None]).astype(jnp.float32)
        local_force = jnp.einsum('ap,cpk->cak', local_hot, terms[:, :LP], precision=lax.Precision.HIGHEST)
        live = rem_c[dev] >= 0
        slot_hot = ((rem_k[dev][None, :] == slot_rows[:, None]) & live[None, :]).astype(jnp.float32)
        slot_force = jnp.einsum('ap,cpk->cak', slot_hot, terms[:, LP:], precision=lax.Precision.HIGHEST)
        return (local_force, slot_force)
    local_all, slot_all = lax.map(device_forces, jnp.arange(N_DOM, dtype=jnp.int32))
    slot_all = slot_all.reshape(N_DOM, 4, ROUNDS, EXP, 128)

    def device_total(dev):
        dst = dev + shifts
        valid = ((dst >= 0) & (dst < N_DOM)).astype(jnp.float32)
        back = slot_all[jnp.clip(dst, 0, N_DOM - 1), :, rounds_idx] * valid[:, None, None, None]
        back = jnp.moveaxis(back, 0, 1).reshape(4, ROUNDS * EXP, 128)
        hot = (exports[dev].reshape(-1)[None, :] == act_rows[:, None]).astype(jnp.float32)
        return local_all[dev] + jnp.einsum('ap,cpk->cak', hot, back, precision=lax.Precision.HIGHEST)
    totals = lax.map(device_total, jnp.arange(N_DOM, dtype=jnp.int32))
    particle_rows = jnp.arange(128, dtype=jnp.int32)
    active = (particle_rows[None, None, :] < active_counts.reshape(N_DOM, ACT)[:, :, None]).astype(jnp.float32)
    accel = totals[:, :3]
    magnitude = jnp.sqrt(lax.optimization_barrier(jnp.sum(accel * accel, axis=1))) * active
    peak = jnp.max(magnitude)
    step = step_max / jnp.sqrt(1.0 + peak / accel_ref)
    accel_flat = jnp.moveaxis(accel, 1, 0).reshape(3, N_DOM * ACT, 128)
    active_flat = active.reshape(N_DOM * ACT, 128)
    kicked = velocities + step * accel_flat * active_flat[None]
    potential = totals[:, 3].reshape(N_DOM * ACT, 128) * active_flat
    return (kicked, potential)
```

```python
import functools

import jax
import jax.numpy as jnp
from jax import lax
from jax.experimental import pallas as pl
from jax.experimental.pallas import tpu as pltpu
from jax.sharding import PartitionSpec as P

MESH = pl.DeviceIdType.MESH

soften_sq = 0.0025
split_coef = 1.1283791670955126
grav_const = 0.001
step_max = 1.0
accel_ref = 0.1

den1, den0, num0, fit_c0, fit_c1, fit_c2 = (
    4.339803588412531,
    5.532797000850757,
    4.3724977862229215,
    0.5635920230826972,
    2.656775940985158,
    6.782305918896453,
)
norm = fit_c2 * num0
shift = 1.0 / num0
fit1 = fit_c1 / fit_c2
fit0 = fit_c0 / fit_c2
coef = split_coef / norm
mass_scale = grav_const * norm
neg_log2e = -1.4426950408889634

ROUNDS, SLOTS, ACT, CELLS, LP, RP = 16, 40, 48, 512, 128, 384
HALF = ROUNDS // 2
OFFSETS = [k + 1 for k in range(HALF)] + [-(k + 1) for k in range(HALF)]
LOW, HIGH = 16, 8
WIDE = 2


def terms(target, source):
    dx, dy, dz = (source[c] - target[c] for c in range(3))
    q = dx * dx + dy * dy + (dz * dz + soften_sq)
    u = lax.rsqrt(q)
    r = q * u
    z = pltpu.reciprocal((q + den0) + den1 * r, approx=True)
    tail = ((z + fit1) * z + fit0) * (z * (u + shift))
    decay = jnp.exp2(q * neg_log2e) * source[3]
    weight = (decay * (tail + coef)) * pltpu.reciprocal(q, approx=True)
    return weight * dx, weight * dy, weight * dz, decay * tail


def pair_group(gathered, rolled):
    source = [gathered[c] for c in range(3)] + [gathered[3] * mass_scale]
    for k in range(16):
        for c in range(4):
            rolled[4 * k + c] = pltpu.roll(source[c], k, 1) if k else source[c]
    target = [gathered[4 + c] for c in range(3)]
    total = None
    for step in range(8):
        turned = [pltpu.roll(t, 16 * step, 1) if step else t for t in target]
        part = None
        for k in range(16):
            term = terms(turned, [rolled[4 * k + c] for c in range(4)])
            part = term if part is None else tuple(a + b for a, b in zip(part, term))
        part = [pltpu.roll(a, 128 - 16 * step, 1) if step else a for a in part]
        total = part if total is None else [a + b for a, b in zip(total, part)]
    return total


def halves(array):
    high = array.astype(jnp.bfloat16)
    low = (array - high.astype(jnp.float32)).astype(jnp.bfloat16)
    return high, low


def picked_sum(hot, array):
    high, low = halves(array)
    return jnp.dot(hot, high, preferred_element_type=jnp.float32) + jnp.dot(
        hot, low, preferred_element_type=jnp.float32
    )


def kernel(
    devices,
    cells_s,
    counts_s,
    ltgt_s,
    lsrc_s,
    exports_s,
    slots_s,
    rcells_s,
    ltgt_v,
    exports_v,
    slots_v,
    rcells_v,
    velocities,
    particles,
    kicked,
    potential,
    sending,
    arrived,
    terms_local,
    terms_remote,
    returning,
    returned,
    own,
    active,
    gathered,
    rolled,
    peaks_low,
    peaks_high,
    send1,
    recv1,
    send2,
    recv2,
    send3,
    recv3,
    send4,
    recv4,
):
    me = lax.axis_index("dom")
    low, high = lax.rem(me, LOW), lax.div(me, LOW)

    def at(by):
        return (lax.rem(me + by + devices, devices),)

    low_peers = [(high * LOW + lax.rem(low + k, LOW),) for k in range(1, LOW)]
    high_peers = [(lax.rem(high + k, HIGH) * LOW + low,) for k in range(1, HIGH)]
    greeted = [at(by) for by in OFFSETS] + low_peers + high_peers
    barrier = pltpu.get_barrier_semaphore()
    for peer in greeted:
        pl.semaphore_signal(barrier, inc=1, device_id=peer, device_id_type=MESH)

    def own_step(a, _):
        cell = cells_s[a]
        for c in range(3):
            own[c, pl.ds(a, 1), :] = particles[c, pl.ds(cell, 1), :]
        return 0

    lax.fori_loop(0, ACT, own_step, 0, unroll=8)

    copies1 = []
    for r in range(ROUNDS):

        def export_step(s, _):
            a = jnp.minimum(exports_s[r, s], ACT - 1)
            for c in range(3):
                sending[r, c, pl.ds(s, 1), :] = own[c, pl.ds(a, 1), :]
            return 0

        lax.fori_loop(0, SLOTS, export_step, 0, unroll=8)
        copies1.append(
            pltpu.make_async_remote_copy(
                src_ref=sending.at[r],
                dst_ref=arrived.at[r],
                send_sem=send1.at[r],
                recv_sem=recv1.at[r],
                device_id=at(OFFSETS[r]),
                device_id_type=MESH,
            )
        )
    pl.semaphore_wait(barrier, len(greeted))
    for copy in copies1:
        copy.start()

    lanes = lax.broadcasted_iota(jnp.int32, (1, 128), 1)

    def active_step(a, _):
        active[pl.ds(a, 1), :] = (lanes < counts_s[a]).astype(jnp.float32)
        return 0

    lax.fori_loop(0, ACT, active_step, 0, unroll=8)

    def local_group(g, _):
        for w in range(WIDE):
            first = (g * WIDE + w) * 8
            for i in range(8):
                cell = lsrc_s[first + i]
                a = ltgt_s[first + i]
                for c in range(4):
                    gathered[w, c, i : i + 1, :] = particles[c, pl.ds(cell, 1), :]
                for c in range(3):
                    gathered[w, 4 + c, i : i + 1, :] = own[c, pl.ds(a, 1), :]
            total = pair_group(gathered.at[w], rolled.at[w])
            for c in range(4):
                terms_local[pl.ds(pl.multiple_of(first, 8), 8), 128 * c : 128 * c + 128] = total[c]
        return 0

    lax.fori_loop(0, LP // 8 // WIDE, local_group, 0)
    for copy in copies1:
        copy.wait()

    def remote_group(g, _):
        for w in range(WIDE):
            first = (g * WIDE + w) * 8
            for i in range(8):
                cell = jnp.maximum(rcells_s[first + i], 0)
                k = slots_s[first + i]
                r = lax.div(k, SLOTS)
                s = k - r * SLOTS
                for c in range(4):
                    gathered[w, c, i : i + 1, :] = particles[c, pl.ds(cell, 1), :]
                for c in range(3):
                    gathered[w, 4 + c, i : i + 1, :] = arrived[r, c, pl.ds(s, 1), :]
            total = pair_group(gathered.at[w], rolled.at[w])
            for c in range(4):
                terms_remote[pl.ds(pl.multiple_of(first, 8), 8), 128 * c : 128 * c + 128] = total[c]
        return 0

    lax.fori_loop(0, RP // 8 // WIDE, remote_group, 0)

    slots = jnp.where(rcells_v[...] >= 0, slots_v[...], -1)
    found_high, found_low = halves(terms_remote[...])
    copies2 = []
    for r in range(ROUNDS):
        rows = lax.broadcasted_iota(jnp.int32, (SLOTS, RP), 0) + r * SLOTS
        hot = (rows == slots).astype(jnp.float32).astype(jnp.bfloat16)
        returning[r] = jnp.dot(hot, found_high, preferred_element_type=jnp.float32) + jnp.dot(
            hot, found_low, preferred_element_type=jnp.float32
        )
        copy = pltpu.make_async_remote_copy(
            src_ref=returning.at[r],
            dst_ref=returned.at[r],
            send_sem=send2.at[r],
            recv_sem=recv2.at[r],
            device_id=at(-OFFSETS[r]),
            device_id_type=MESH,
        )
        copy.start()
        copies2.append(copy)

    hot = (lax.broadcasted_iota(jnp.int32, (ACT, LP), 0) == ltgt_v[...]).astype(jnp.float32)
    total = picked_sum(hot.astype(jnp.bfloat16), terms_local[...])
    for r in range(ROUNDS):
        rows = lax.broadcasted_iota(jnp.int32, (ACT, SLOTS), 0)
        hot = (rows == exports_v[r : r + 1, :]).astype(jnp.float32)
        copies2[r].wait()
        total = total + picked_sum(hot.astype(jnp.bfloat16), returned[r])

    live = active[...]
    accel = [total[:, 128 * c : 128 * c + 128] * live for c in range(3)]
    size = accel[0] * accel[0] + accel[1] * accel[1] + accel[2] * accel[2]
    top = size[0:8]
    for k in range(1, ACT // 8):
        top = jnp.maximum(top, size[8 * k : 8 * k + 8])
    for peaks, peers, send, recv in (
        (peaks_low, low_peers, send3, recv3),
        (peaks_high, high_peers, send4, recv4),
    ):
        peaks[0] = top
        copies = []
        for k, peer in enumerate(peers):
            copy = pltpu.make_async_remote_copy(
                src_ref=peaks.at[0],
                dst_ref=peaks.at[k + 1],
                send_sem=send.at[k],
                recv_sem=recv.at[k],
                device_id=peer,
                device_id_type=MESH,
            )
            copy.start()
            copies.append(copy)
        for copy in copies:
            copy.wait()
        for k in range(len(peers)):
            top = jnp.maximum(top, peaks[k + 1])
    peak = jnp.sqrt(jnp.max(top, axis=(0, 1), keepdims=True))
    step = step_max / jnp.sqrt(1.0 + peak / accel_ref)
    for c in range(3):
        kicked[c] = velocities[c] + step * accel[c]
    potential[...] = -(total[:, 384:512] * live)


def shards(
    particles,
    velocities,
    active_cells,
    active_counts,
    local_targets,
    local_sources,
    export_lists,
    remote_slots,
    remote_cells,
):
    smem = pl.BlockSpec(memory_space=pltpu.SMEM)
    vmem = pl.BlockSpec(memory_space=pltpu.VMEM)
    dma = pltpu.SemaphoreType.DMA
    f32 = jnp.float32
    return pl.pallas_call(
        functools.partial(kernel, lax.axis_size("dom")),
        out_shape=(
            jax.ShapeDtypeStruct((3, ACT, 128), f32),
            jax.ShapeDtypeStruct((ACT, 128), f32),
        ),
        in_specs=[smem] * 7 + [vmem] * 6,
        out_specs=(vmem, vmem),
        scratch_shapes=[
            pltpu.VMEM((ROUNDS, 3, SLOTS, 128), f32),
            pltpu.VMEM((ROUNDS, 3, SLOTS, 128), f32),
            pltpu.VMEM((LP, 512), f32),
            pltpu.VMEM((RP, 512), f32),
            pltpu.VMEM((ROUNDS, SLOTS, 512), f32),
            pltpu.VMEM((ROUNDS, SLOTS, 512), f32),
            pltpu.VMEM((3, ACT, 128), f32),
            pltpu.VMEM((ACT, 128), f32),
            pltpu.VMEM((WIDE, 7, 8, 128), f32),
            pltpu.VMEM((WIDE, 64, 8, 128), f32),
            pltpu.VMEM((LOW, 8, 128), f32),
            pltpu.VMEM((HIGH, 8, 128), f32),
            dma((ROUNDS,)),
            dma((ROUNDS,)),
            dma((ROUNDS,)),
            dma((ROUNDS,)),
            dma((LOW - 1,)),
            dma((LOW - 1,)),
            dma((HIGH - 1,)),
            dma((HIGH - 1,)),
        ],
        compiler_params=pltpu.CompilerParams(
            collective_id=0, has_side_effects=True, vmem_limit_bytes=32 * 1024 * 1024
        ),
    )(
        active_cells,
        active_counts,
        local_targets,
        local_sources,
        export_lists,
        remote_slots,
        remote_cells,
        local_targets.reshape(1, LP),
        export_lists,
        remote_slots.reshape(1, RP),
        remote_cells.reshape(1, RP),
        velocities,
        particles,
    )


def solution(mesh):
    return jax.shard_map(
        shards,
        mesh=mesh,
        in_specs=(
            P(None, "dom", None),
            P(None, "dom", None),
            P("dom"),
            P("dom"),
            P("dom"),
            P("dom"),
            P("dom", None),
            P("dom"),
            P("dom"),
        ),
        out_specs=(P(None, "dom", None), P("dom", None)),
        check_vma=False,
    )
```

```python
import functools

import jax
import jax.numpy as jnp
from jax import lax
from jax.experimental import pallas as pl
from jax.experimental.pallas import tpu as pltpu
from jax.sharding import PartitionSpec as P

MESH = pl.DeviceIdType.MESH

soften_sq = 0.0025
split_coef = 1.1283791670955126
grav_const = 0.001
step_max = 1.0
accel_ref = 0.1

den1, den0, num0, fit_c0, fit_c1, fit_c2 = (
    4.339803588412531,
    5.532797000850757,
    4.3724977862229215,
    0.5635920230826972,
    2.656775940985158,
    6.782305918896453,
)
norm = fit_c2 * num0
shift = 1.0 / num0
fit1 = fit_c1 / fit_c2
fit0 = fit_c0 / fit_c2
coef = split_coef / norm
mass_scale = grav_const * norm
neg_log2e = -1.4426950408889634

ROUNDS, SLOTS, ACT, CELLS, LP, RP = 16, 40, 48, 512, 128, 384
HALF = ROUNDS // 2
OFFSETS = [k + 1 for k in range(HALF)] + [-(k + 1) for k in range(HALF)]
ORDER = [7, 15, 1, 9, 6, 14, 2, 10, 5, 13, 3, 11, 0, 8, 4, 12]
LOW, HIGH = 8, 16
CHUNK, UNROLL = 32, 64
CHUNKS = 128 // CHUNK
BATCHES = RP // 128


def terms(target, source):
    dx, dy, dz = (source[c] - target[c] for c in range(3))
    q = dx * dx + dy * dy + (dz * dz + soften_sq)
    u = lax.rsqrt(q)
    r = q * u
    z = pltpu.reciprocal((q + den0) + den1 * r, approx=True)
    tail = ((z + fit1) * z + fit0) * (z * (u + shift))
    decay = jnp.exp2(q * neg_log2e) * source[3]
    weight = (decay * (tail + coef)) * pltpu.reciprocal(q, approx=True)
    return weight * dx, weight * dy, weight * dz, decay * tail


def pair_block(sources, targets, batch, first):
    blocks = CHUNK // 8
    target = [[targets[batch, c, pl.ds(first + 8 * k, 8), :] for c in range(3)] for k in range(blocks)]

    def some(step, sums):
        sums = [list(a) for a in sums]
        for j in range(UNROLL):
            row = step * UNROLL + j
            source = [
                jnp.broadcast_to(sources[batch, c, pl.ds(row, 1), :], (8, 128)) for c in range(4)
            ]
            for k in range(blocks):
                sums[k] = [a + b for a, b in zip(sums[k], terms(target[k], source))]
        return tuple(tuple(a) for a in sums)

    zero = jnp.zeros((8, 128), jnp.float32)
    return lax.fori_loop(0, 128 // UNROLL, some, ((zero,) * 4,) * blocks)


def halves(array):
    high = array.astype(jnp.bfloat16)
    low = (array - high.astype(jnp.float32)).astype(jnp.bfloat16)
    return high, low


def picked_sum(hot, array, axis):
    width = array.shape[1 - axis]
    both = jnp.concatenate(halves(array), axis=1 - axis)
    dims = (((1,), (axis,)), ((), ()))
    both = lax.dot_general(hot, both, dims, preferred_element_type=jnp.float32)
    return both[:, :width] + both[:, width:]


def one_hot(rows, picks):
    return (rows == picks).astype(jnp.float32).astype(jnp.bfloat16)


def kernel(
    devices,
    cells_h,
    counts_h,
    ltgt_h,
    lsrc_h,
    exports_h,
    slots_h,
    rcells_h,
    ltgt_row_h,
    slots_rows_h,
    rcells_rows_h,
    velocities_h,
    particles_h,
    kicked,
    potential,
    cells_s,
    counts_s,
    ltgt_s,
    lsrc_s,
    exports_s,
    slots_s,
    rcells_s,
    exports_v,
    ltgt_v,
    slots_v,
    rcells_v,
    velocities,
    particles,
    rows_s,
    load_sem,
    sending,
    arrived,
    terms_local,
    terms_remote,
    returning,
    returned,
    active,
    gathered,
    sources,
    targets,
    slot_hot,
    export_hot,
    peaks_low,
    peaks_high,
    send1,
    recv1,
    send2,
    recv2,
    send3,
    recv3,
    send4,
    recv4,
):
    me = lax.axis_index("dom")
    low, high = lax.rem(me, LOW), lax.div(me, LOW)

    def at(by):
        return (lax.rem(me + by + devices, devices),)

    low_peers = [(high * LOW + lax.rem(low + k, LOW),) for k in range(1, LOW)]
    high_peers = [(lax.rem(high + k, HIGH) * LOW + low,) for k in range(1, HIGH)]
    greeted = [at(by) for by in OFFSETS] + low_peers + high_peers
    barrier = pltpu.get_barrier_semaphore()
    for peer in greeted:
        pl.semaphore_signal(barrier, inc=1, device_id=peer, device_id_type=MESH)

    loads = [
        pltpu.make_async_copy(source, place, load_sem.at[k])
        for k, (source, place) in enumerate(
            (
                (particles_h, particles),
                (cells_h, cells_s),
                (exports_h, exports_s),
                (ltgt_h, ltgt_s),
                (lsrc_h, lsrc_s),
                (counts_h, counts_s),
                (slots_h, slots_s),
                (rcells_h, rcells_s),
                (exports_h, exports_v),
                (ltgt_row_h, ltgt_v),
                (slots_rows_h, slots_v),
                (rcells_rows_h, rcells_v),
                (velocities_h, velocities),
            )
        )
    ]
    for load in loads:
        load.start()
    for load in loads[:3]:
        load.wait()

    def sent_copy(r):
        return pltpu.make_async_remote_copy(
            src_ref=sending.at[r],
            dst_ref=arrived.at[pl.ds(r * 3 * SLOTS, 3 * SLOTS)],
            send_sem=send1.at[r],
            recv_sem=recv1.at[r],
            device_id=at(OFFSETS[r]),
            device_id_type=MESH,
        )

    for r in ORDER:

        def export_step(s, _):
            cell = cells_s[jnp.minimum(exports_s[r, s], ACT - 1)]
            for c in range(3):
                sending[r, pl.ds(c * SLOTS + s, 1), :] = particles[c, pl.ds(cell, 1), :]
            return 0

        lax.fori_loop(0, SLOTS, export_step, 0, unroll=8)
    pl.semaphore_wait(barrier, len(greeted))
    for r in ORDER:
        sent_copy(r).start()
    for load in loads[3:]:
        load.wait()

    lanes = lax.broadcasted_iota(jnp.int32, (1, 128), 1)

    def active_step(a, _):
        active[pl.ds(a, 1), :] = (lanes < counts_s[a]).astype(jnp.float32)
        return 0

    lax.fori_loop(0, ACT, active_step, 0, unroll=8)

    def gather_sources(batch, cell_of):
        def pair(p, _):
            cell = cell_of(p)
            for c in range(4):
                gathered[c, pl.ds(p, 1), :] = particles[c, pl.ds(cell, 1), :]
            return 0

        lax.fori_loop(0, 128, pair, 0, unroll=8)
        for c in range(3):
            sources[batch, c] = gathered[c].T
        sources[batch, 3] = gathered[3].T * mass_scale

    def local_target(p, _):
        cell = cells_s[ltgt_s[p]]
        for c in range(3):
            gathered[c, pl.ds(p, 1), :] = particles[c, pl.ds(cell, 1), :]
        return 0

    lax.fori_loop(0, 128, local_target, 0, unroll=8)
    for c in range(3):
        targets[0, c] = gathered[c].T
    gather_sources(0, lambda p: lsrc_s[p])
    for b in range(BATCHES):
        gather_sources(b + 1, lambda p: jnp.maximum(rcells_s[128 * b + p], 0))

    def local_chunk(q, _):
        found = pair_block(sources, targets, 0, pl.multiple_of(q * CHUNK, CHUNK))
        for k in range(CHUNK // 8):
            for c in range(4):
                terms_local[q, c * CHUNK + 8 * k : c * CHUNK + 8 * k + 8, :] = found[k][c]
        return 0

    lax.fori_loop(0, CHUNKS, local_chunk, 0)

    slots = jnp.where(rcells_v[...] >= 0, slots_v[...], -1)
    slots = jnp.concatenate([slots[k : k + 1] for k in range(BATCHES)], axis=1)
    for k in range(ROUNDS * SLOTS // 128):
        rows = lax.broadcasted_iota(jnp.int32, (128, RP), 0) + 128 * k
        slot_hot[128 * k : 128 * k + 128, :] = one_hot(rows, slots)
    rows = lax.broadcasted_iota(jnp.int32, (ACT, ROUNDS * SLOTS), 0)
    lists = jnp.concatenate([exports_v[r : r + 1, :] for r in range(ROUNDS)], axis=1)
    export_hot[...] = one_hot(rows, lists)

    def place_row(p, _):
        k = slots_s[p]
        rows_s[p] = k + lax.div(k, SLOTS) * (2 * SLOTS)
        return 0

    lax.fori_loop(0, RP, place_row, 0, unroll=8)
    for r in ORDER:
        sent_copy(r).wait()

    for b in range(BATCHES):

        def remote_target(p, _):
            row = rows_s[128 * b + p]
            for c in range(3):
                gathered[c, pl.ds(p, 1), :] = arrived[pl.ds(row + c * SLOTS, 1), :]
            return 0

        lax.fori_loop(0, 128, remote_target, 0, unroll=8)
        for c in range(3):
            targets[b + 1, c] = gathered[c].T

    def return_copy(q, r):
        return pltpu.make_async_remote_copy(
            src_ref=returning.at[q, r],
            dst_ref=returned.at[q, r],
            send_sem=send2.at[q, r],
            recv_sem=recv2.at[q, r],
            device_id=at(-OFFSETS[r]),
            device_id_type=MESH,
        )

    def remote_chunk(q, _):
        def batch(b, _):
            found = pair_block(sources, targets, b + 1, pl.multiple_of(q * CHUNK, CHUNK))
            for k in range(CHUNK // 8):
                for c in range(4):
                    terms_remote[b, c * CHUNK + 8 * k : c * CHUNK + 8 * k + 8, :] = found[k][c]
            return 0

        lax.fori_loop(0, BATCHES, batch, 0)
        found = jnp.concatenate([terms_remote[b] for b in range(BATCHES)], axis=1)
        back = picked_sum(slot_hot[...], found, 1)
        for r in range(ROUNDS):
            returning[q, r] = back[SLOTS * r : SLOTS * r + SLOTS]
        for r in ORDER:
            return_copy(q, r).start()
        return 0

    lax.fori_loop(0, CHUNKS, remote_chunk, 0)

    local_hot = one_hot(lax.broadcasted_iota(jnp.int32, (ACT, LP), 0), ltgt_v[...])
    totals = []
    for q in range(CHUNKS):
        total = picked_sum(local_hot, terms_local[q], 1)
        for r in ORDER:
            return_copy(q, r).wait()
        back = jnp.concatenate([returned[q, r] for r in range(ROUNDS)], axis=0)
        totals.append(total + picked_sum(export_hot[...], back, 0))
    total = jnp.concatenate(
        [totals[q][:, CHUNK * c : CHUNK * c + CHUNK] for c in range(4) for q in range(CHUNKS)], axis=1
    )

    live = active[...]
    accel = [total[:, 128 * c : 128 * c + 128] * live for c in range(3)]
    size = accel[0] * accel[0] + accel[1] * accel[1] + accel[2] * accel[2]
    top = size[0:8]
    for k in range(1, ACT // 8):
        top = jnp.maximum(top, size[8 * k : 8 * k + 8])
    top = jnp.max(top, axis=0, keepdims=True)
    for peaks, peers, send, recv in (
        (peaks_low, low_peers, send3, recv3),
        (peaks_high, high_peers, send4, recv4),
    ):
        peaks[0] = top
        copies = []
        for k, peer in enumerate(peers):
            copy = pltpu.make_async_remote_copy(
                src_ref=peaks.at[0],
                dst_ref=peaks.at[k + 1],
                send_sem=send.at[k],
                recv_sem=recv.at[k],
                device_id=peer,
                device_id_type=MESH,
            )
            copy.start()
            copies.append(copy)
        for copy in copies:
            copy.wait()
        for k in range(len(peers)):
            top = jnp.maximum(top, peaks[k + 1])
    peak = jnp.sqrt(jnp.max(top, axis=(0, 1), keepdims=True))
    step = step_max / jnp.sqrt(1.0 + peak / accel_ref)
    for c in range(3):
        kicked[c] = velocities[c] + step * accel[c]
    potential[...] = -(total[:, 384:512] * live)


def shards(
    particles,
    velocities,
    active_cells,
    active_counts,
    local_targets,
    local_sources,
    export_lists,
    remote_slots,
    remote_cells,
):
    hbm = pl.BlockSpec(memory_space=pltpu.HBM)
    vmem = pl.BlockSpec(memory_space=pltpu.VMEM)
    dma = pltpu.SemaphoreType.DMA
    f32, i32 = jnp.float32, jnp.int32
    return pl.pallas_call(
        functools.partial(kernel, lax.axis_size("dom")),
        out_shape=(
            jax.ShapeDtypeStruct((3, ACT, 128), f32),
            jax.ShapeDtypeStruct((ACT, 128), f32),
        ),
        in_specs=[hbm] * 12,
        out_specs=(vmem, vmem),
        scratch_shapes=[
            pltpu.SMEM((ACT,), i32),
            pltpu.SMEM((ACT,), i32),
            pltpu.SMEM((LP,), i32),
            pltpu.SMEM((LP,), i32),
            pltpu.SMEM((ROUNDS, SLOTS), i32),
            pltpu.SMEM((RP,), i32),
            pltpu.SMEM((RP,), i32),
            pltpu.VMEM((ROUNDS, SLOTS), i32),
            pltpu.VMEM((1, LP), i32),
            pltpu.VMEM((RP // 128, 128), i32),
            pltpu.VMEM((RP // 128, 128), i32),
            pltpu.VMEM((3, ACT, 128), f32),
            pltpu.VMEM((4, CELLS, 128), f32),
            pltpu.SMEM((RP,), i32),
            dma((13,)),
            pltpu.VMEM((ROUNDS, 3 * SLOTS, 128), f32),
            pltpu.VMEM((ROUNDS * 3 * SLOTS, 128), f32),
            pltpu.VMEM((CHUNKS, 128, 128), f32),
            pltpu.VMEM((BATCHES, 128, 128), f32),
            pltpu.VMEM((CHUNKS, ROUNDS, SLOTS, 128), f32),
            pltpu.VMEM((CHUNKS, ROUNDS, SLOTS, 128), f32),
            pltpu.VMEM((ACT, 128), f32),
            pltpu.VMEM((4, 128, 128), f32),
            pltpu.VMEM((1 + BATCHES, 4, 128, 128), f32),
            pltpu.VMEM((1 + BATCHES, 3, 128, 128), f32),
            pltpu.VMEM((ROUNDS * SLOTS, RP), jnp.bfloat16),
            pltpu.VMEM((ACT, ROUNDS * SLOTS), jnp.bfloat16),
            pltpu.VMEM((LOW, 1, 128), f32),
            pltpu.VMEM((HIGH, 1, 128), f32),
            dma((ROUNDS,)),
            dma((ROUNDS,)),
            dma((CHUNKS, ROUNDS)),
            dma((CHUNKS, ROUNDS)),
            dma((LOW - 1,)),
            dma((LOW - 1,)),
            dma((HIGH - 1,)),
            dma((HIGH - 1,)),
        ],
        compiler_params=pltpu.CompilerParams(
            collective_id=0, has_side_effects=True, vmem_limit_bytes=63 * 1024 * 1024
        ),
    )(
        active_cells,
        active_counts,
        local_targets,
        local_sources,
        export_lists,
        remote_slots,
        remote_cells,
        local_targets.reshape(1, LP),
        remote_slots.reshape(RP // 128, 128),
        remote_cells.reshape(RP // 128, 128),
        velocities,
        particles,
    )


def solution(mesh):
    return jax.shard_map(
        shards,
        mesh=mesh,
        in_specs=(
            P(None, "dom", None),
            P(None, "dom", None),
            P("dom"),
            P("dom"),
            P("dom"),
            P("dom"),
            P("dom", None),
            P("dom"),
            P("dom"),
        ),
        out_specs=(P(None, "dom", None), P("dom", None)),
        check_vma=False,
    )
```

```python
import functools

import jax
import jax.numpy as jnp
from jax import lax
from jax.experimental import pallas as pl
from jax.experimental.pallas import tpu as pltpu
from jax.sharding import PartitionSpec as P

MESH = pl.DeviceIdType.MESH

soften_sq = 0.0025
split_coef = 1.1283791670955126
grav_const = 0.001
step_max = 1.0
accel_ref = 0.1

den1, den0, num0, fit_c0, fit_c1, fit_c2 = (
    4.339803588412531,
    5.532797000850757,
    4.3724977862229215,
    0.5635920230826972,
    2.656775940985158,
    6.782305918896453,
)
scale = (fit_c2 * num0 / split_coef) ** (1.0 / 3.0)
shift = 1.0 / num0
fit1 = fit_c1 / fit_c2 * scale
fit0 = fit_c0 / fit_c2 * scale * scale
mass_scale = grav_const * split_coef
neg_log2e = -1.4426950408889634

ROUNDS, SLOTS, ACT, CELLS, LP, RP = 16, 40, 48, 512, 128, 384
HALF = ROUNDS // 2
OFFSETS = [k + 1 for k in range(HALF)] + [-(k + 1) for k in range(HALF)]
ORDER = [7, 15, 1, 9, 6, 14, 2, 10, 5, 13, 3, 11, 0, 8, 4, 12]
LOW, HIGH = 8, 16
CHUNK, UNROLL = 32, 64
CHUNKS = 128 // CHUNK
BATCHES = RP // 128
SIDE = SLOTS // 2
SENT = 64
EARLY = 2
PHASES = [(0, 2), (2, 1), (3, 1)]


def terms(target, source):
    dx, dy, dz = (source[c] - target[c] for c in range(3))
    q = dx * dx + dy * dy + (dz * dz + soften_sq)
    u = lax.rsqrt(q)
    z = pltpu.reciprocal((u * (den1 / scale) + 1.0 / scale) * q + den0 / scale, approx=True)
    tail = ((z + fit1) * z + fit0) * (z * (u + shift))
    decay = jnp.exp2(q * neg_log2e) * source[3]
    pull = decay * tail
    weight = (pull + decay) * (u * u)
    return weight * dx, weight * dy, weight * dz, pull


def pair_block(sources, targets, batch, first):
    blocks = CHUNK // 8
    target = [[targets[batch, c, pl.ds(first + 8 * k, 8), :] for c in range(3)] for k in range(blocks)]

    def some(step, sums):
        sums = [list(a) for a in sums]
        for j in range(UNROLL):
            row = step * UNROLL + j
            source = [
                jnp.broadcast_to(sources[batch, c, pl.ds(row, 1), :], (8, 128)) for c in range(4)
            ]
            for k in range(blocks):
                sums[k] = [a + b for a, b in zip(sums[k], terms(target[k], source))]
        return tuple(tuple(a) for a in sums)

    zero = jnp.zeros((8, 128), jnp.float32)
    return lax.fori_loop(0, 128 // UNROLL, some, ((zero,) * 4,) * blocks)


def halves(array):
    high = array.astype(jnp.bfloat16)
    low = (array - high.astype(jnp.float32)).astype(jnp.bfloat16)
    return high, low


def picked_sum(hot, array, axis):
    width = array.shape[1 - axis]
    both = jnp.concatenate(halves(array), axis=1 - axis)
    dims = (((1,), (axis,)), ((), ()))
    both = lax.dot_general(hot, both, dims, preferred_element_type=jnp.float32)
    return both[:, :width] + both[:, width:]


def one_hot(rows, picks):
    return (rows == picks).astype(jnp.float32).astype(jnp.bfloat16)


def kernel(
    devices,
    cells_h,
    counts_h,
    ltgt_h,
    lsrc_h,
    exports_h,
    slots_h,
    rcells_h,
    ltgt_row_h,
    slots_rows_h,
    rcells_rows_h,
    velocities_h,
    particles_h,
    kicked,
    potential,
    cells_s,
    counts_s,
    ltgt_s,
    lsrc_s,
    exports_s,
    slots_s,
    rcells_s,
    exports_v,
    ltgt_v,
    slots_v,
    rcells_v,
    velocities,
    particles,
    rows_s,
    rows_v,
    load_sem,
    exported,
    sending,
    arrived_first,
    arrived_second,
    picked,
    terms_local,
    terms_remote,
    returning,
    returned,
    active,
    gathered,
    sources,
    targets,
    slot_hot,
    export_hot,
    peaks_low,
    peaks_high,
    send1,
    recv1,
    send2,
    recv2,
    send3,
    recv3,
    send4,
    recv4,
):
    me = lax.axis_index("dom")
    low, high = lax.rem(me, LOW), lax.div(me, LOW)

    def at(by):
        return (lax.rem(me + by + devices, devices),)

    low_peers = [(high * LOW + lax.rem(low + k, LOW),) for k in range(1, LOW)]
    high_peers = [(lax.rem(high + k, HIGH) * LOW + low,) for k in range(1, HIGH)]
    greeted = [at(by) for by in OFFSETS] + low_peers + high_peers
    barrier = pltpu.get_barrier_semaphore()

    loads = [
        pltpu.make_async_copy(source, place, load_sem.at[k])
        for k, (source, place) in enumerate(
            (
                (particles_h, particles),
                (cells_h, cells_s),
                (exports_h, exports_s),
                (ltgt_h, ltgt_s),
                (lsrc_h, lsrc_s),
                (counts_h, counts_s),
                (slots_h, slots_s),
                (rcells_h, rcells_s),
                (exports_h, exports_v),
                (ltgt_row_h, ltgt_v),
                (slots_rows_h, slots_v),
                (rcells_rows_h, rcells_v),
                (velocities_h, velocities),
            )
        )
    ]
    for load in loads[:3]:
        load.start()
    for peer in greeted:
        pl.semaphore_signal(barrier, inc=1, device_id=peer, device_id_type=MESH)
    for load in loads[3:]:
        load.start()
    for load in loads[:3]:
        load.wait()

    arrived = (arrived_first, arrived_second)

    def sent_copy(h, r):
        return pltpu.make_async_remote_copy(
            src_ref=sending.at[h, r],
            dst_ref=arrived[h].at[pl.ds(r * SENT, SENT)],
            send_sem=send1.at[h, r],
            recv_sem=recv1.at[h, r],
            device_id=at(OFFSETS[r]),
            device_id_type=MESH,
        )

    first_half = lax.broadcasted_iota(jnp.int32, (1, 128), 1) < 64

    def both_halves(a, b):
        return (
            jnp.where(first_half, a, pltpu.roll(b, 64, 1)),
            jnp.where(first_half, pltpu.roll(a, 64, 1), b),
        )

    def export_round(r, _):
        for s in range(SLOTS):
            cell = cells_s[jnp.minimum(exports_s[r, s], ACT - 1)]
            for c in range(3):
                row = s if c < 2 or s < SIDE else s + 4
                exported[r, c, row : row + 1, :] = particles[c, pl.ds(cell, 1), :]
        return 0

    lax.fori_loop(0, ROUNDS, export_round, 0)
    for r in ORDER:
        xy = both_halves(exported[r, 0, 0:SLOTS], exported[r, 1, 0:SLOTS])
        zz = both_halves(exported[r, 2, 0:SIDE], exported[r, 2, SIDE + 4 : SLOTS + 4])
        for h in range(2):
            sending[h, r, 0:SLOTS] = xy[h]
            sending[h, r, SLOTS : SLOTS + SIDE] = zz[h]
            sending[h, r, SLOTS + SIDE : SENT] = jnp.zeros((SENT - SLOTS - SIDE, 128), jnp.float32)
    pl.semaphore_wait(barrier, len(greeted))
    for h in range(2):
        for r in ORDER:
            sent_copy(h, r).start()
    for load in loads[3:]:
        load.wait()

    slots = slots_v[...]
    rounds = lax.shift_right_logical(slots * 1639, 16)
    slots = slots - rounds * SLOTS
    turned = slots >= SIDE
    rows_v[0:BATCHES] = rounds * SENT + slots
    rows_v[4 : 4 + BATCHES] = rounds * SENT + SLOTS + jnp.where(turned, slots - SIDE, slots)
    rows_copy = pltpu.make_async_copy(rows_v, rows_s, load_sem.at[13])
    rows_copy.start()

    lanes = lax.broadcasted_iota(jnp.int32, (1, 128), 1)

    def active_step(a, _):
        active[pl.ds(a, 1), :] = (lanes < counts_s[a]).astype(jnp.float32)
        return 0

    lax.fori_loop(0, ACT, active_step, 0, unroll=8)

    def local_pair(p, _):
        place = pl.ds(p, 1)
        cell = cells_s[ltgt_s[p]]
        for c in range(3):
            picked[c, place, :] = particles[c, pl.ds(cell, 1), :]
        cell = lsrc_s[p]
        for c in range(4):
            gathered[c, place, :] = particles[c, pl.ds(cell, 1), :]
        return 0

    def remote_source(p, _):
        place = pl.ds(128 + p, 1)
        cell = jnp.maximum(rcells_s[p], 0)
        for c in range(4):
            gathered[c, place, :] = particles[c, pl.ds(cell, 1), :]
        return 0

    lax.fori_loop(0, LP, local_pair, 0, unroll=16)
    lax.fori_loop(0, RP, remote_source, 0, unroll=16)
    for c in range(3):
        targets[0, c] = picked[c, 0:128].T
    for b in range(1 + BATCHES):
        for c in range(3):
            sources[b, c] = gathered[c, 128 * b : 128 * b + 128].T
        sources[b, 3] = gathered[3, 128 * b : 128 * b + 128].T * mass_scale

    def local_chunk(q, _):
        found = pair_block(sources, targets, 0, pl.multiple_of(q * CHUNK, CHUNK))
        for k in range(CHUNK // 8):
            for c in range(4):
                terms_local[q, c * CHUNK + 8 * k : c * CHUNK + 8 * k + 8, :] = found[k][c]
        return 0

    lax.fori_loop(0, EARLY, local_chunk, 0)

    slots = jnp.where(rcells_v[...] >= 0, slots_v[...], -1)
    slots = jnp.concatenate([slots[k : k + 1] for k in range(BATCHES)], axis=1)
    for k in range(ROUNDS * SLOTS // 128):
        rows = lax.broadcasted_iota(jnp.int32, (128, RP), 0) + 128 * k
        slot_hot[128 * k : 128 * k + 128, :] = one_hot(rows, slots)
    rows = lax.broadcasted_iota(jnp.int32, (ACT, ROUNDS * SLOTS), 0)
    lists = jnp.concatenate([exports_v[r : r + 1, :] for r in range(ROUNDS)], axis=1)
    export_hot[...] = one_hot(rows, lists)

    rows_copy.wait()

    def take_targets(h):
        for r in ORDER:
            sent_copy(h, r).wait()

        for b in range(BATCHES):

            def remote_target(p, _):
                place = pl.ds(128 * b + p, 1)
                picked[0, place, :] = arrived[h][pl.ds(rows_s[b, p], 1), :]
                picked[1, place, :] = arrived[h][pl.ds(rows_s[4 + b, p], 1), :]
                return 0

            lax.fori_loop(0, 128, remote_target, 0, unroll=32)
        for b in range(BATCHES):
            xy = picked[0, 128 * b : 128 * b + 128].T
            zz = picked[1, 128 * b : 128 * b + 128].T
            targets[b + 1, 0, 64 * h : 64 * h + 64] = xy[:64]
            targets[b + 1, 1, 64 * h : 64 * h + 64] = xy[64:]
            targets[b + 1, 2, 64 * h : 64 * h + 64] = jnp.where(turned[b : b + 1], zz[64:], zz[:64])

    def return_copy(phase, r):
        first, count = PHASES[phase]
        return pltpu.make_async_remote_copy(
            src_ref=returning.at[r, first : first + count],
            dst_ref=returned.at[r, first : first + count],
            send_sem=send2.at[phase, r],
            recv_sem=recv2.at[phase, r],
            device_id=at(-OFFSETS[r]),
            device_id_type=MESH,
        )

    def remote_chunk(q, _):
        def batch(b, _):
            found = pair_block(sources, targets, b + 1, pl.multiple_of(q * CHUNK, CHUNK))
            for k in range(CHUNK // 8):
                for c in range(4):
                    terms_remote[b, c * CHUNK + 8 * k : c * CHUNK + 8 * k + 8, :] = found[k][c]
            return 0

        lax.fori_loop(0, BATCHES, batch, 0)
        found = jnp.concatenate([terms_remote[b] for b in range(BATCHES)], axis=1)
        back = picked_sum(slot_hot[...], found, 1)
        for r in range(ROUNDS):
            returning[r, q] = back[SLOTS * r : SLOTS * r + SLOTS]
        return 0

    for phase, (first, count) in enumerate(PHASES):
        if phase < 2:
            take_targets(phase)
        lax.fori_loop(first, first + count, remote_chunk, 0)
        for r in ORDER:
            return_copy(phase, r).start()
    lax.fori_loop(EARLY, CHUNKS, local_chunk, 0)

    local_hot = one_hot(lax.broadcasted_iota(jnp.int32, (ACT, LP), 0), ltgt_v[...])
    totals = []
    for q in range(CHUNKS):
        total = picked_sum(local_hot, terms_local[q], 1)
        for phase, (first, _) in enumerate(PHASES):
            if q == first:
                for r in ORDER:
                    return_copy(phase, r).wait()
        back = jnp.concatenate([returned[r, q] for r in range(ROUNDS)], axis=0)
        totals.append(total + picked_sum(export_hot[...], back, 0))
    total = jnp.concatenate(
        [totals[q][:, CHUNK * c : CHUNK * c + CHUNK] for c in range(4) for q in range(CHUNKS)], axis=1
    )

    live = active[...]
    accel = [total[:, 128 * c : 128 * c + 128] * live for c in range(3)]
    size = accel[0] * accel[0] + accel[1] * accel[1] + accel[2] * accel[2]
    top = size[0:8]
    for k in range(1, ACT // 8):
        top = jnp.maximum(top, size[8 * k : 8 * k + 8])
    top = jnp.max(top, axis=0, keepdims=True)
    for peaks, peers, send, recv in (
        (peaks_low, low_peers, send3, recv3),
        (peaks_high, high_peers, send4, recv4),
    ):
        peaks[0] = top
        copies = []
        for k, peer in enumerate(peers):
            copy = pltpu.make_async_remote_copy(
                src_ref=peaks.at[0],
                dst_ref=peaks.at[k + 1],
                send_sem=send.at[k],
                recv_sem=recv.at[k],
                device_id=peer,
                device_id_type=MESH,
            )
            copy.start()
            copies.append(copy)
        for copy in copies:
            copy.wait()
        for k in range(len(peers)):
            top = jnp.maximum(top, peaks[k + 1])
    peak = jnp.sqrt(jnp.max(top, axis=(0, 1), keepdims=True))
    step = step_max / jnp.sqrt(1.0 + peak / accel_ref)
    for c in range(3):
        kicked[c] = velocities[c] + step * accel[c]
    potential[...] = -(total[:, 384:512] * live)


def shards(
    particles,
    velocities,
    active_cells,
    active_counts,
    local_targets,
    local_sources,
    export_lists,
    remote_slots,
    remote_cells,
):
    hbm = pl.BlockSpec(memory_space=pltpu.HBM)
    vmem = pl.BlockSpec(memory_space=pltpu.VMEM)
    dma = pltpu.SemaphoreType.DMA
    f32, i32 = jnp.float32, jnp.int32
    return pl.pallas_call(
        functools.partial(kernel, lax.axis_size("dom")),
        out_shape=(
            jax.ShapeDtypeStruct((3, ACT, 128), f32),
            jax.ShapeDtypeStruct((ACT, 128), f32),
        ),
        in_specs=[hbm] * 12,
        out_specs=(vmem, vmem),
        scratch_shapes=[
            pltpu.SMEM((ACT,), i32),
            pltpu.SMEM((ACT,), i32),
            pltpu.SMEM((LP,), i32),
            pltpu.SMEM((LP,), i32),
            pltpu.SMEM((ROUNDS, SLOTS), i32),
            pltpu.SMEM((RP,), i32),
            pltpu.SMEM((RP,), i32),
            pltpu.VMEM((ROUNDS, SLOTS), i32),
            pltpu.VMEM((1, LP), i32),
            pltpu.VMEM((RP // 128, 128), i32),
            pltpu.VMEM((RP // 128, 128), i32),
            pltpu.VMEM((3, ACT, 128), f32),
            pltpu.VMEM((4, CELLS, 128), f32),
            pltpu.SMEM((8, 128), i32),
            pltpu.VMEM((8, 128), i32),
            dma((14,)),
            pltpu.VMEM((ROUNDS, 3, 48, 128), f32),
            pltpu.VMEM((2, ROUNDS, SENT, 128), f32),
            pltpu.VMEM((ROUNDS * SENT, 128), f32),
            pltpu.VMEM((ROUNDS * SENT, 128), f32),
            pltpu.VMEM((3, RP, 128), f32),
            pltpu.VMEM((CHUNKS, 128, 128), f32),
            pltpu.VMEM((BATCHES, 128, 128), f32),
            pltpu.VMEM((ROUNDS, CHUNKS, SLOTS, 128), f32),
            pltpu.VMEM((ROUNDS, CHUNKS, SLOTS, 128), f32),
            pltpu.VMEM((ACT, 128), f32),
            pltpu.VMEM((4, LP + RP, 128), f32),
            pltpu.VMEM((1 + BATCHES, 4, 128, 128), f32),
            pltpu.VMEM((1 + BATCHES, 3, 128, 128), f32),
            pltpu.VMEM((ROUNDS * SLOTS, RP), jnp.bfloat16),
            pltpu.VMEM((ACT, ROUNDS * SLOTS), jnp.bfloat16),
            pltpu.VMEM((LOW, 1, 128), f32),
            pltpu.VMEM((HIGH, 1, 128), f32),
            dma((2, ROUNDS)),
            dma((2, ROUNDS)),
            dma((len(PHASES), ROUNDS)),
            dma((len(PHASES), ROUNDS)),
            dma((LOW - 1,)),
            dma((LOW - 1,)),
            dma((HIGH - 1,)),
            dma((HIGH - 1,)),
        ],
        compiler_params=pltpu.CompilerParams(
            collective_id=0, has_side_effects=True, vmem_limit_bytes=63 * 1024 * 1024
        ),
    )(
        active_cells,
        active_counts,
        local_targets,
        local_sources,
        export_lists,
        remote_slots,
        remote_cells,
        local_targets.reshape(1, LP),
        remote_slots.reshape(RP // 128, 128),
        remote_cells.reshape(RP // 128, 128),
        velocities,
        particles,
    )


def solution(mesh):
    return jax.shard_map(
        shards,
        mesh=mesh,
        in_specs=(
            P(None, "dom", None),
            P(None, "dom", None),
            P("dom"),
            P("dom"),
            P("dom"),
            P("dom"),
            P("dom", None),
            P("dom"),
            P("dom"),
        ),
        out_specs=(P(None, "dom", None), P("dom", None)),
        check_vma=False,
    )
```

```python
import functools

import jax
import jax.numpy as jnp
from jax import lax
from jax.experimental import pallas as pl
from jax.experimental.pallas import tpu as pltpu
from jax.sharding import PartitionSpec as P

MESH = pl.DeviceIdType.MESH

soften_sq = 0.0025
split_coef = 1.1283791670955126
grav_const = 0.001
step_max = 1.0
accel_ref = 0.1

den1, den0, num0, fit_c0, fit_c1, fit_c2 = (
    4.339803588412531,
    5.532797000850757,
    4.3724977862229215,
    0.5635920230826972,
    2.656775940985158,
    6.782305918896453,
)
scale = (fit_c2 * num0 / split_coef) ** (1.0 / 3.0)
shift = 1.0 / num0
fit1 = fit_c1 / fit_c2 * scale
fit0 = fit_c0 / fit_c2 * scale * scale
mass_scale = grav_const * split_coef
neg_log2e = -1.4426950408889634

ROUNDS, SLOTS, ACT, CELLS, LP, RP = 16, 40, 48, 512, 128, 384
HALF = ROUNDS // 2
OFFSETS = [k + 1 for k in range(HALF)] + [-(k + 1) for k in range(HALF)]
ORDER = [7, 15, 1, 9, 6, 14, 2, 10, 5, 13, 3, 11, 0, 8, 4, 12]
LOW, HIGH = 8, 16
CHUNK, UNROLL = 32, 64
CHUNKS = 128 // CHUNK
BATCHES = RP // 128
SIDE = SLOTS // 2
SENT = 64
EARLY = 2
PHASES = [(0, 2), (2, 1), (3, 1)]


def terms(target, source):
    dx, dy, dz = (source[c] - target[c] for c in range(3))
    q = dx * dx + dy * dy + (dz * dz + soften_sq)
    u = lax.rsqrt(q)
    z = pltpu.reciprocal((u * (den1 / scale) + 1.0 / scale) * q + den0 / scale, approx=True)
    tail = ((z + fit1) * z + fit0) * (z * (u + shift))
    decay = jnp.exp2(q * neg_log2e) * source[3]
    pull = decay * tail
    weight = (pull + decay) * (u * u)
    return weight * dx, weight * dy, weight * dz, pull


def pair_block(sources, targets, batch, first):
    blocks = CHUNK // 8
    target = [[targets[batch, c, pl.ds(first + 8 * k, 8), :] for c in range(3)] for k in range(blocks)]

    def some(step, sums):
        sums = [list(a) for a in sums]
        for j in range(UNROLL):
            row = step * UNROLL + j
            source = [
                jnp.broadcast_to(sources[batch, c, pl.ds(row, 1), :], (8, 128)) for c in range(4)
            ]
            for k in range(blocks):
                sums[k] = [a + b for a, b in zip(sums[k], terms(target[k], source))]
        return tuple(tuple(a) for a in sums)

    zero = jnp.zeros((8, 128), jnp.float32)
    return lax.fori_loop(0, 128 // UNROLL, some, ((zero,) * 4,) * blocks)


def halves(array):
    high = array.astype(jnp.bfloat16)
    low = (array - high.astype(jnp.float32)).astype(jnp.bfloat16)
    return high, low


def picked_sum(hot, array, axis):
    width = array.shape[1 - axis]
    both = jnp.concatenate(halves(array), axis=1 - axis)
    dims = (((1,), (axis,)), ((), ()))
    both = lax.dot_general(hot, both, dims, preferred_element_type=jnp.float32)
    return both[:, :width] + both[:, width:]


def one_hot(rows, picks):
    return (rows == picks).astype(jnp.float32).astype(jnp.bfloat16)


def kernel(
    devices,
    cells_h,
    counts_h,
    ltgt_h,
    lsrc_h,
    exports_h,
    slots_h,
    rcells_h,
    ltgt_row_h,
    slots_rows_h,
    rcells_rows_h,
    velocities_h,
    particles_h,
    kicked,
    potential,
    cells_s,
    counts_s,
    ltgt_s,
    lsrc_s,
    exports_s,
    slots_s,
    rcells_s,
    exports_v,
    ltgt_v,
    slots_v,
    rcells_v,
    velocities,
    particles,
    rows_s,
    rows_v,
    load_sem,
    exported,
    sending,
    arrived_first,
    arrived_second,
    picked,
    terms_local,
    terms_remote,
    returning,
    returned,
    active,
    gathered,
    sources,
    targets,
    slot_hot,
    export_hot,
    peaks_low,
    peaks_high,
    send1,
    recv1,
    send2,
    recv2,
    send3,
    recv3,
    send4,
    recv4,
):
    me = lax.axis_index("dom")
    low, high = lax.rem(me, LOW), lax.div(me, LOW)

    def at(by):
        return (lax.rem(me + by + devices, devices),)

    low_peers = [(high * LOW + lax.rem(low + k, LOW),) for k in range(1, LOW)]
    high_peers = [(lax.rem(high + k, HIGH) * LOW + low,) for k in range(1, HIGH)]
    greeted = [at(by) for by in OFFSETS] + low_peers + high_peers
    barrier = pltpu.get_barrier_semaphore()

    loads = [
        pltpu.make_async_copy(source, place, load_sem.at[k])
        for k, (source, place) in enumerate(
            (
                (particles_h, particles),
                (cells_h, cells_s),
                (exports_h, exports_s),
                (ltgt_h, ltgt_s),
                (lsrc_h, lsrc_s),
                (counts_h, counts_s),
                (slots_h, slots_s),
                (rcells_h, rcells_s),
                (exports_h, exports_v),
                (ltgt_row_h, ltgt_v),
                (slots_rows_h, slots_v),
                (rcells_rows_h, rcells_v),
                (velocities_h, velocities),
            )
        )
    ]
    for load in loads[:3]:
        load.start()
    for peer in greeted:
        pl.semaphore_signal(barrier, inc=1, device_id=peer, device_id_type=MESH)
    for load in loads[3:]:
        load.start()
    for load in loads[:3]:
        load.wait()

    arrived = (arrived_first, arrived_second)

    def sent_copy(h, r):
        return pltpu.make_async_remote_copy(
            src_ref=sending.at[h, r],
            dst_ref=arrived[h].at[pl.ds(r * SENT, SENT)],
            send_sem=send1.at[h, r],
            recv_sem=recv1.at[h, r],
            device_id=at(OFFSETS[r]),
            device_id_type=MESH,
        )

    first_half = lax.broadcasted_iota(jnp.int32, (1, 128), 1) < 64

    def both_halves(a, b):
        return (
            jnp.where(first_half, a, pltpu.roll(b, 64, 1)),
            jnp.where(first_half, pltpu.roll(a, 64, 1), b),
        )

    for r in ORDER:

        def export_slot(s, _):
            cell = cells_s[jnp.minimum(exports_s[r, s], ACT - 1)]
            for c in range(2):
                exported[r, c, pl.ds(s, 1), :] = particles[c, pl.ds(cell, 1), :]
            gap = 4 * lax.div(s, SIDE)
            exported[r, 2, pl.ds(s + gap, 1), :] = particles[2, pl.ds(cell, 1), :]
            return 0

        lax.fori_loop(0, SLOTS, export_slot, 0, unroll=True)

    def pack(h):
        for r in ORDER:
            xy = both_halves(exported[r, 0, 0:SLOTS], exported[r, 1, 0:SLOTS])
            zz = both_halves(exported[r, 2, 0:SIDE], exported[r, 2, SIDE + 4 : SLOTS + 4])
            sending[h, r, 0:SLOTS] = xy[h]
            sending[h, r, SLOTS : SLOTS + SIDE] = zz[h]
            sending[h, r, SLOTS + SIDE : SENT] = jnp.zeros((SENT - SLOTS - SIDE, 128), jnp.float32)

    pack(0)
    pl.semaphore_wait(barrier, len(greeted))
    for r in ORDER:
        sent_copy(0, r).start()
    pack(1)
    for r in ORDER:
        sent_copy(1, r).start()
    for load in loads[3:]:
        load.wait()

    slots = slots_v[...]
    rounds = lax.shift_right_logical(slots * 1639, 16)
    slots = slots - rounds * SLOTS
    turned = slots >= SIDE
    rows_v[0:BATCHES] = rounds * SENT + slots
    rows_v[8 : 8 + BATCHES] = jnp.maximum(rcells_v[...], 0)
    rows_v[4 : 4 + BATCHES] = rounds * SENT + SLOTS + jnp.where(turned, slots - SIDE, slots)
    rows_copy = pltpu.make_async_copy(rows_v, rows_s, load_sem.at[13])
    rows_copy.start()

    lanes = lax.broadcasted_iota(jnp.int32, (1, 128), 1)

    def active_step(a, _):
        active[pl.ds(a, 1), :] = (lanes < counts_s[a]).astype(jnp.float32)
        return 0

    lax.fori_loop(0, ACT, active_step, 0, unroll=8)

    def local_pair(p, _):
        place = pl.ds(p, 1)
        cell = cells_s[ltgt_s[p]]
        for c in range(3):
            picked[c, place, :] = particles[c, pl.ds(cell, 1), :]
        cell = lsrc_s[p]
        for c in range(4):
            gathered[c, place, :] = particles[c, pl.ds(cell, 1), :]
        return 0

    lax.fori_loop(0, LP, local_pair, 0, unroll=True)
    rows_copy.wait()
    for b in range(BATCHES):

        def remote_source(p, _):
            place = pl.ds(128 * (b + 1) + p, 1)
            cell = rows_s[8 + b, p]
            for c in range(4):
                gathered[c, place, :] = particles[c, pl.ds(cell, 1), :]
            return 0

        lax.fori_loop(0, 128, remote_source, 0, unroll=True)
    for c in range(3):
        targets[0, c] = picked[c, 0:128].T
    for b in range(1 + BATCHES):
        for c in range(3):
            sources[b, c] = gathered[c, 128 * b : 128 * b + 128].T
        sources[b, 3] = gathered[3, 128 * b : 128 * b + 128].T * mass_scale

    def local_chunk(q, _):
        found = pair_block(sources, targets, 0, pl.multiple_of(q * CHUNK, CHUNK))
        for k in range(CHUNK // 8):
            for c in range(4):
                terms_local[q, c * CHUNK + 8 * k : c * CHUNK + 8 * k + 8, :] = found[k][c]
        return 0

    lax.fori_loop(0, EARLY, local_chunk, 0)

    slots = jnp.where(rcells_v[...] >= 0, slots_v[...], -1)
    slots = jnp.concatenate([slots[k : k + 1] for k in range(BATCHES)], axis=1)
    for k in range(ROUNDS * SLOTS // 128):
        rows = lax.broadcasted_iota(jnp.int32, (128, RP), 0) + 128 * k
        slot_hot[128 * k : 128 * k + 128, :] = one_hot(rows, slots)
    rows = lax.broadcasted_iota(jnp.int32, (ACT, ROUNDS * SLOTS), 0)
    lists = jnp.concatenate([exports_v[r : r + 1, :] for r in range(ROUNDS)], axis=1)
    export_hot[...] = one_hot(rows, lists)

    def take_targets(h):
        for r in ORDER:
            sent_copy(h, r).wait()

        for b in range(BATCHES):

            def remote_target(p, _):
                place = pl.ds(128 * b + p, 1)
                picked[0, place, :] = arrived[h][pl.ds(rows_s[b, p], 1), :]
                picked[1, place, :] = arrived[h][pl.ds(rows_s[4 + b, p], 1), :]
                return 0

            lax.fori_loop(0, 128, remote_target, 0, unroll=True)
        for b in range(BATCHES):
            xy = picked[0, 128 * b : 128 * b + 128].T
            zz = picked[1, 128 * b : 128 * b + 128].T
            targets[b + 1, 0, 64 * h : 64 * h + 64] = xy[:64]
            targets[b + 1, 1, 64 * h : 64 * h + 64] = xy[64:]
            targets[b + 1, 2, 64 * h : 64 * h + 64] = jnp.where(turned[b : b + 1], zz[64:], zz[:64])

    def return_copy(phase, r):
        first, count = PHASES[phase]
        return pltpu.make_async_remote_copy(
            src_ref=returning.at[r, first : first + count],
            dst_ref=returned.at[r, first : first + count],
            send_sem=send2.at[phase, r],
            recv_sem=recv2.at[phase, r],
            device_id=at(-OFFSETS[r]),
            device_id_type=MESH,
        )

    def remote_chunk(q, _):
        def batch(b, _):
            found = pair_block(sources, targets, b + 1, pl.multiple_of(q * CHUNK, CHUNK))
            for k in range(CHUNK // 8):
                for c in range(4):
                    terms_remote[b, c * CHUNK + 8 * k : c * CHUNK + 8 * k + 8, :] = found[k][c]
            return 0

        lax.fori_loop(0, BATCHES, batch, 0)
        found = jnp.concatenate([terms_remote[b] for b in range(BATCHES)], axis=1)
        back = picked_sum(slot_hot[...], found, 1)
        for r in range(ROUNDS):
            returning[r, q] = back[SLOTS * r : SLOTS * r + SLOTS]
        return 0

    for phase, (first, count) in enumerate(PHASES):
        if phase < 2:
            take_targets(phase)
        lax.fori_loop(first, first + count, remote_chunk, 0)
        for r in ORDER:
            return_copy(phase, r).start()
    lax.fori_loop(EARLY, CHUNKS, local_chunk, 0)

    local_hot = one_hot(lax.broadcasted_iota(jnp.int32, (ACT, LP), 0), ltgt_v[...])
    totals = []
    for q in range(CHUNKS):
        total = picked_sum(local_hot, terms_local[q], 1)
        for phase, (first, _) in enumerate(PHASES):
            if q == first:
                for r in ORDER:
                    return_copy(phase, r).wait()
        back = jnp.concatenate([returned[r, q] for r in range(ROUNDS)], axis=0)
        totals.append(total + picked_sum(export_hot[...], back, 0))
    total = jnp.concatenate(
        [totals[q][:, CHUNK * c : CHUNK * c + CHUNK] for c in range(4) for q in range(CHUNKS)], axis=1
    )

    live = active[...]
    accel = [total[:, 128 * c : 128 * c + 128] * live for c in range(3)]
    size = accel[0] * accel[0] + accel[1] * accel[1] + accel[2] * accel[2]
    top = size[0:8]
    for k in range(1, ACT // 8):
        top = jnp.maximum(top, size[8 * k : 8 * k + 8])
    top = jnp.max(top, axis=0, keepdims=True)
    for peaks, peers, send, recv in (
        (peaks_low, low_peers, send3, recv3),
        (peaks_high, high_peers, send4, recv4),
    ):
        peaks[0] = top
        copies = []
        for k, peer in enumerate(peers):
            copy = pltpu.make_async_remote_copy(
                src_ref=peaks.at[0],
                dst_ref=peaks.at[k + 1],
                send_sem=send.at[k],
                recv_sem=recv.at[k],
                device_id=peer,
                device_id_type=MESH,
            )
            copy.start()
            copies.append(copy)
        for copy in copies:
            copy.wait()
        for k in range(len(peers)):
            top = jnp.maximum(top, peaks[k + 1])
    peak = jnp.sqrt(jnp.max(top, axis=(0, 1), keepdims=True))
    step = step_max / jnp.sqrt(1.0 + peak / accel_ref)
    for c in range(3):
        kicked[c] = velocities[c] + step * accel[c]
    potential[...] = -(total[:, 384:512] * live)


def shards(
    particles,
    velocities,
    active_cells,
    active_counts,
    local_targets,
    local_sources,
    export_lists,
    remote_slots,
    remote_cells,
):
    hbm = pl.BlockSpec(memory_space=pltpu.HBM)
    vmem = pl.BlockSpec(memory_space=pltpu.VMEM)
    dma = pltpu.SemaphoreType.DMA
    f32, i32 = jnp.float32, jnp.int32
    return pl.pallas_call(
        functools.partial(kernel, lax.axis_size("dom")),
        out_shape=(
            jax.ShapeDtypeStruct((3, ACT, 128), f32),
            jax.ShapeDtypeStruct((ACT, 128), f32),
        ),
        in_specs=[hbm] * 12,
        out_specs=(vmem, vmem),
        scratch_shapes=[
            pltpu.SMEM((ACT,), i32),
            pltpu.SMEM((ACT,), i32),
            pltpu.SMEM((LP,), i32),
            pltpu.SMEM((LP,), i32),
            pltpu.SMEM((ROUNDS, SLOTS), i32),
            pltpu.SMEM((RP,), i32),
            pltpu.SMEM((RP,), i32),
            pltpu.VMEM((ROUNDS, SLOTS), i32),
            pltpu.VMEM((1, LP), i32),
            pltpu.VMEM((RP // 128, 128), i32),
            pltpu.VMEM((RP // 128, 128), i32),
            pltpu.VMEM((3, ACT, 128), f32),
            pltpu.VMEM((4, CELLS, 128), f32),
            pltpu.SMEM((16, 128), i32),
            pltpu.VMEM((16, 128), i32),
            dma((14,)),
            pltpu.VMEM((ROUNDS, 3, 48, 128), f32),
            pltpu.VMEM((2, ROUNDS, SENT, 128), f32),
            pltpu.VMEM((ROUNDS * SENT, 128), f32),
            pltpu.VMEM((ROUNDS * SENT, 128), f32),
            pltpu.VMEM((3, RP, 128), f32),
            pltpu.VMEM((CHUNKS, 128, 128), f32),
            pltpu.VMEM((BATCHES, 128, 128), f32),
            pltpu.VMEM((ROUNDS, CHUNKS, SLOTS, 128), f32),
            pltpu.VMEM((ROUNDS, CHUNKS, SLOTS, 128), f32),
            pltpu.VMEM((ACT, 128), f32),
            pltpu.VMEM((4, LP + RP, 128), f32),
            pltpu.VMEM((1 + BATCHES, 4, 128, 128), f32),
            pltpu.VMEM((1 + BATCHES, 3, 128, 128), f32),
            pltpu.VMEM((ROUNDS * SLOTS, RP), jnp.bfloat16),
            pltpu.VMEM((ACT, ROUNDS * SLOTS), jnp.bfloat16),
            pltpu.VMEM((LOW, 1, 128), f32),
            pltpu.VMEM((HIGH, 1, 128), f32),
            dma((2, ROUNDS)),
            dma((2, ROUNDS)),
            dma((len(PHASES), ROUNDS)),
            dma((len(PHASES), ROUNDS)),
            dma((LOW - 1,)),
            dma((LOW - 1,)),
            dma((HIGH - 1,)),
            dma((HIGH - 1,)),
        ],
        compiler_params=pltpu.CompilerParams(
            collective_id=0, has_side_effects=True, vmem_limit_bytes=63 * 1024 * 1024
        ),
    )(
        active_cells,
        active_counts,
        local_targets,
        local_sources,
        export_lists,
        remote_slots,
        remote_cells,
        local_targets.reshape(1, LP),
        remote_slots.reshape(RP // 128, 128),
        remote_cells.reshape(RP // 128, 128),
        velocities,
        particles,
    )


def solution(mesh):
    return jax.shard_map(
        shards,
        mesh=mesh,
        in_specs=(
            P(None, "dom", None),
            P(None, "dom", None),
            P("dom"),
            P("dom"),
            P("dom"),
            P("dom"),
            P("dom", None),
            P("dom"),
            P("dom"),
        ),
        out_specs=(P(None, "dom", None), P("dom", None)),
        check_vma=False,
    )
```

```python
import functools

import jax
import jax.numpy as jnp
from jax import lax
from jax.experimental import pallas as pl
from jax.experimental.pallas import tpu as pltpu
from jax.sharding import PartitionSpec as P

MESH = pl.DeviceIdType.MESH

soften_sq = 0.0025
split_coef = 1.1283791670955126
grav_const = 0.001
step_max = 1.0
accel_ref = 0.1

den1, den0, fit_c1, shift, fit_c2, fit_c0 = (
    3.536723577677721,
    3.6889203995886692,
    0.3283891689702059,
    0.2475050952121036,
    6.153377939151487,
    0.010250218214333296,
)
scale = (fit_c2 / split_coef) ** 0.5
fit1 = fit_c1 * scale
fit0 = fit_c0 * scale
mass_scale = grav_const * split_coef
neg_log2e = -1.4426950408889634

ROUNDS, SLOTS, ACT, CELLS, LP, RP = 16, 40, 48, 512, 128, 384
HALF = ROUNDS // 2
OFFSETS = [k + 1 for k in range(HALF)] + [-(k + 1) for k in range(HALF)]
ORDER = [7, 15, 1, 9, 6, 14, 2, 10, 5, 13, 3, 11, 0, 8, 4, 12]
LOW, HIGH = 8, 16
CHUNK, UNROLL = 32, 64
CHUNKS = 128 // CHUNK
BATCHES = RP // 128
SIDE = SLOTS // 2
SENT = 64
EARLY = 2
PHASES = [(0, 2), (2, 1), (3, 1)]


def terms(target, source):
    dx, dy, dz = (source[c] - target[c] for c in range(3))
    q = dx * dx + dy * dy + (dz * dz + soften_sq)
    u = lax.rsqrt(q)
    z = pltpu.reciprocal((u * (den1 / scale) + 1.0 / scale) * q + den0 / scale, approx=True)
    tail = ((u + shift) * (z + fit1) + fit0) * z
    decay = jnp.exp2(q * neg_log2e) * source[3]
    pull = decay * tail
    weight = (pull + decay) * (u * u)
    return weight * dx, weight * dy, weight * dz, pull


def pair_block(sources, targets, batch, first):
    blocks = CHUNK // 8
    target = [[targets[batch, c, pl.ds(first + 8 * k, 8), :] for c in range(3)] for k in range(blocks)]

    def some(step, sums):
        sums = [list(a) for a in sums]
        for j in range(UNROLL):
            row = step * UNROLL + j
            source = [
                jnp.broadcast_to(sources[batch, c, pl.ds(row, 1), :], (8, 128)) for c in range(4)
            ]
            for k in range(blocks):
                sums[k] = [a + b for a, b in zip(sums[k], terms(target[k], source))]
        return tuple(tuple(a) for a in sums)

    zero = jnp.zeros((8, 128), jnp.float32)
    return lax.fori_loop(0, 128 // UNROLL, some, ((zero,) * 4,) * blocks)


def halves(array):
    high = array.astype(jnp.bfloat16)
    low = (array - high.astype(jnp.float32)).astype(jnp.bfloat16)
    return high, low


def picked_sum(hot, array, axis):
    width = array.shape[1 - axis]
    both = jnp.concatenate(halves(array), axis=1 - axis)
    dims = (((1,), (axis,)), ((), ()))
    both = lax.dot_general(hot, both, dims, preferred_element_type=jnp.float32)
    return both[:, :width] + both[:, width:]


def one_hot(rows, picks):
    return (rows == picks).astype(jnp.float32).astype(jnp.bfloat16)


def kernel(
    devices,
    cells_h,
    counts_h,
    ltgt_h,
    lsrc_h,
    exports_h,
    slots_h,
    rcells_h,
    ltgt_row_h,
    slots_rows_h,
    rcells_rows_h,
    velocities_h,
    particles_h,
    kicked,
    potential,
    cells_s,
    counts_s,
    ltgt_s,
    lsrc_s,
    exports_s,
    slots_s,
    rcells_s,
    exports_v,
    ltgt_v,
    slots_v,
    rcells_v,
    velocities,
    particles,
    rows_s,
    rows_v,
    load_sem,
    exported,
    sending,
    arrived_first,
    arrived_second,
    picked,
    terms_local,
    terms_remote,
    returning,
    returned,
    active,
    gathered,
    sources,
    targets,
    slot_hot,
    export_hot,
    peaks_low,
    peaks_high,
    send1,
    recv1,
    send2,
    recv2,
    send3,
    recv3,
    send4,
    recv4,
):
    me = lax.axis_index("dom")
    low, high = lax.rem(me, LOW), lax.div(me, LOW)

    def at(by):
        return (lax.rem(me + by + devices, devices),)

    low_peers = [(high * LOW + lax.rem(low + k, LOW),) for k in range(1, LOW)]
    high_peers = [(lax.rem(high + k, HIGH) * LOW + low,) for k in range(1, HIGH)]
    greeted = [at(by) for by in OFFSETS] + low_peers + high_peers
    barrier = pltpu.get_barrier_semaphore()

    loads = [
        pltpu.make_async_copy(source, place, load_sem.at[k])
        for k, (source, place) in enumerate(
            (
                (particles_h, particles),
                (cells_h, cells_s),
                (exports_h, exports_s),
                (ltgt_h, ltgt_s),
                (lsrc_h, lsrc_s),
                (counts_h, counts_s),
                (slots_h, slots_s),
                (rcells_h, rcells_s),
                (exports_h, exports_v),
                (ltgt_row_h, ltgt_v),
                (slots_rows_h, slots_v),
                (rcells_rows_h, rcells_v),
                (velocities_h, velocities),
            )
        )
    ]
    for load in loads[:3]:
        load.start()
    for peer in greeted:
        pl.semaphore_signal(barrier, inc=1, device_id=peer, device_id_type=MESH)
    for load in loads[3:]:
        load.start()
    for load in loads[:3]:
        load.wait()

    arrived = (arrived_first, arrived_second)

    def sent_copy(h, r):
        return pltpu.make_async_remote_copy(
            src_ref=sending.at[h, r],
            dst_ref=arrived[h].at[pl.ds(r * SENT, SENT)],
            send_sem=send1.at[h, r],
            recv_sem=recv1.at[h, r],
            device_id=at(OFFSETS[r]),
            device_id_type=MESH,
        )

    first_half = lax.broadcasted_iota(jnp.int32, (1, 128), 1) < 64

    def both_halves(a, b):
        return (
            jnp.where(first_half, a, pltpu.roll(b, 64, 1)),
            jnp.where(first_half, pltpu.roll(a, 64, 1), b),
        )

    for r in ORDER:

        def export_slot(s, _):
            cell = cells_s[jnp.minimum(exports_s[r, s], ACT - 1)]
            for c in range(2):
                exported[r, c, pl.ds(s, 1), :] = particles[c, pl.ds(cell, 1), :]
            gap = 4 * lax.div(s, SIDE)
            exported[r, 2, pl.ds(s + gap, 1), :] = particles[2, pl.ds(cell, 1), :]
            return 0

        lax.fori_loop(0, SLOTS, export_slot, 0, unroll=True)

    def pack(h):
        for r in ORDER:
            xy = both_halves(exported[r, 0, 0:SLOTS], exported[r, 1, 0:SLOTS])
            zz = both_halves(exported[r, 2, 0:SIDE], exported[r, 2, SIDE + 4 : SLOTS + 4])
            sending[h, r, 0:SLOTS] = xy[h]
            sending[h, r, SLOTS : SLOTS + SIDE] = zz[h]
            sending[h, r, SLOTS + SIDE : SENT] = jnp.zeros((SENT - SLOTS - SIDE, 128), jnp.float32)

    pack(0)
    pl.semaphore_wait(barrier, len(greeted))
    for r in ORDER:
        sent_copy(0, r).start()
    pack(1)
    for r in ORDER:
        sent_copy(1, r).start()
    for load in loads[3:]:
        load.wait()

    slots = slots_v[...]
    rounds = lax.shift_right_logical(slots * 1639, 16)
    slots = slots - rounds * SLOTS
    turned = slots >= SIDE
    rows_v[0:BATCHES] = rounds * SENT + slots
    rows_v[8 : 8 + BATCHES] = jnp.maximum(rcells_v[...], 0)
    rows_v[4 : 4 + BATCHES] = rounds * SENT + SLOTS + jnp.where(turned, slots - SIDE, slots)
    rows_copy = pltpu.make_async_copy(rows_v, rows_s, load_sem.at[13])
    rows_copy.start()

    lanes = lax.broadcasted_iota(jnp.int32, (1, 128), 1)

    def active_step(a, _):
        active[pl.ds(a, 1), :] = (lanes < counts_s[a]).astype(jnp.float32)
        return 0

    lax.fori_loop(0, ACT, active_step, 0, unroll=8)

    def local_pair(p, _):
        place = pl.ds(p, 1)
        cell = cells_s[ltgt_s[p]]
        for c in range(3):
            picked[c, place, :] = particles[c, pl.ds(cell, 1), :]
        cell = lsrc_s[p]
        for c in range(4):
            gathered[c, place, :] = particles[c, pl.ds(cell, 1), :]
        return 0

    lax.fori_loop(0, LP, local_pair, 0, unroll=True)
    rows_copy.wait()
    for b in range(BATCHES):

        def remote_source(p, _):
            place = pl.ds(128 * (b + 1) + p, 1)
            cell = rows_s[8 + b, p]
            for c in range(4):
                gathered[c, place, :] = particles[c, pl.ds(cell, 1), :]
            return 0

        lax.fori_loop(0, 128, remote_source, 0, unroll=True)
    for c in range(3):
        targets[0, c] = picked[c, 0:128].T
    for b in range(1 + BATCHES):
        for c in range(3):
            sources[b, c] = gathered[c, 128 * b : 128 * b + 128].T
        sources[b, 3] = gathered[3, 128 * b : 128 * b + 128].T * mass_scale

    def local_chunk(q, _):
        found = pair_block(sources, targets, 0, pl.multiple_of(q * CHUNK, CHUNK))
        for k in range(CHUNK // 8):
            for c in range(4):
                terms_local[q, c * CHUNK + 8 * k : c * CHUNK + 8 * k + 8, :] = found[k][c]
        return 0

    lax.fori_loop(0, EARLY, local_chunk, 0)

    slots = jnp.where(rcells_v[...] >= 0, slots_v[...], -1)
    slots = jnp.concatenate([slots[k : k + 1] for k in range(BATCHES)], axis=1)
    for k in range(ROUNDS * SLOTS // 128):
        rows = lax.broadcasted_iota(jnp.int32, (128, RP), 0) + 128 * k
        slot_hot[128 * k : 128 * k + 128, :] = one_hot(rows, slots)
    rows = lax.broadcasted_iota(jnp.int32, (ACT, ROUNDS * SLOTS), 0)
    lists = jnp.concatenate([exports_v[r : r + 1, :] for r in range(ROUNDS)], axis=1)
    export_hot[...] = one_hot(rows, lists)

    def take_targets(h):
        for r in ORDER:
            sent_copy(h, r).wait()

        for b in range(BATCHES):

            def remote_target(p, _):
                place = pl.ds(128 * b + p, 1)
                picked[0, place, :] = arrived[h][pl.ds(rows_s[b, p], 1), :]
                picked[1, place, :] = arrived[h][pl.ds(rows_s[4 + b, p], 1), :]
                return 0

            lax.fori_loop(0, 128, remote_target, 0, unroll=True)
        for b in range(BATCHES):
            xy = picked[0, 128 * b : 128 * b + 128].T
            zz = picked[1, 128 * b : 128 * b + 128].T
            targets[b + 1, 0, 64 * h : 64 * h + 64] = xy[:64]
            targets[b + 1, 1, 64 * h : 64 * h + 64] = xy[64:]
            targets[b + 1, 2, 64 * h : 64 * h + 64] = jnp.where(turned[b : b + 1], zz[64:], zz[:64])

    def return_copy(phase, r):
        first, count = PHASES[phase]
        return pltpu.make_async_remote_copy(
            src_ref=returning.at[r, first : first + count],
            dst_ref=returned.at[r, first : first + count],
            send_sem=send2.at[phase, r],
            recv_sem=recv2.at[phase, r],
            device_id=at(-OFFSETS[r]),
            device_id_type=MESH,
        )

    def remote_chunk(q, _):
        def batch(b, _):
            found = pair_block(sources, targets, b + 1, pl.multiple_of(q * CHUNK, CHUNK))
            for k in range(CHUNK // 8):
                for c in range(4):
                    terms_remote[b, c * CHUNK + 8 * k : c * CHUNK + 8 * k + 8, :] = found[k][c]
            return 0

        lax.fori_loop(0, BATCHES, batch, 0)
        found = jnp.concatenate([terms_remote[b] for b in range(BATCHES)], axis=1)
        back = picked_sum(slot_hot[...], found, 1)
        for r in range(ROUNDS):
            returning[r, q] = back[SLOTS * r : SLOTS * r + SLOTS]
        return 0

    for phase, (first, count) in enumerate(PHASES):
        if phase < 2:
            take_targets(phase)
        lax.fori_loop(first, first + count, remote_chunk, 0)
        for r in ORDER:
            return_copy(phase, r).start()
    lax.fori_loop(EARLY, CHUNKS, local_chunk, 0)

    local_hot = one_hot(lax.broadcasted_iota(jnp.int32, (ACT, LP), 0), ltgt_v[...])
    totals = []
    for q in range(CHUNKS):
        total = picked_sum(local_hot, terms_local[q], 1)
        for phase, (first, _) in enumerate(PHASES):
            if q == first:
                for r in ORDER:
                    return_copy(phase, r).wait()
        back = jnp.concatenate([returned[r, q] for r in range(ROUNDS)], axis=0)
        totals.append(total + picked_sum(export_hot[...], back, 0))
    total = jnp.concatenate(
        [totals[q][:, CHUNK * c : CHUNK * c + CHUNK] for c in range(4) for q in range(CHUNKS)], axis=1
    )

    live = active[...]
    accel = [total[:, 128 * c : 128 * c + 128] * live for c in range(3)]
    size = accel[0] * accel[0] + accel[1] * accel[1] + accel[2] * accel[2]
    top = size[0:8]
    for k in range(1, ACT // 8):
        top = jnp.maximum(top, size[8 * k : 8 * k + 8])
    top = jnp.max(top, axis=0, keepdims=True)
    for peaks, peers, send, recv in (
        (peaks_low, low_peers, send3, recv3),
        (peaks_high, high_peers, send4, recv4),
    ):
        peaks[0] = top
        copies = []
        for k, peer in enumerate(peers):
            copy = pltpu.make_async_remote_copy(
                src_ref=peaks.at[0],
                dst_ref=peaks.at[k + 1],
                send_sem=send.at[k],
                recv_sem=recv.at[k],
                device_id=peer,
                device_id_type=MESH,
            )
            copy.start()
            copies.append(copy)
        for copy in copies:
            copy.wait()
        for k in range(len(peers)):
            top = jnp.maximum(top, peaks[k + 1])
    peak = jnp.sqrt(jnp.max(top, axis=(0, 1), keepdims=True))
    step = step_max / jnp.sqrt(1.0 + peak / accel_ref)
    for c in range(3):
        kicked[c] = velocities[c] + step * accel[c]
    potential[...] = -(total[:, 384:512] * live)


def shards(
    particles,
    velocities,
    active_cells,
    active_counts,
    local_targets,
    local_sources,
    export_lists,
    remote_slots,
    remote_cells,
):
    hbm = pl.BlockSpec(memory_space=pltpu.HBM)
    vmem = pl.BlockSpec(memory_space=pltpu.VMEM)
    dma = pltpu.SemaphoreType.DMA
    f32, i32 = jnp.float32, jnp.int32
    return pl.pallas_call(
        functools.partial(kernel, lax.axis_size("dom")),
        out_shape=(
            jax.ShapeDtypeStruct((3, ACT, 128), f32),
            jax.ShapeDtypeStruct((ACT, 128), f32),
        ),
        in_specs=[hbm] * 12,
        out_specs=(vmem, vmem),
        scratch_shapes=[
            pltpu.SMEM((ACT,), i32),
            pltpu.SMEM((ACT,), i32),
            pltpu.SMEM((LP,), i32),
            pltpu.SMEM((LP,), i32),
            pltpu.SMEM((ROUNDS, SLOTS), i32),
            pltpu.SMEM((RP,), i32),
            pltpu.SMEM((RP,), i32),
            pltpu.VMEM((ROUNDS, SLOTS), i32),
            pltpu.VMEM((1, LP), i32),
            pltpu.VMEM((RP // 128, 128), i32),
            pltpu.VMEM((RP // 128, 128), i32),
            pltpu.VMEM((3, ACT, 128), f32),
            pltpu.VMEM((4, CELLS, 128), f32),
            pltpu.SMEM((16, 128), i32),
            pltpu.VMEM((16, 128), i32),
            dma((14,)),
            pltpu.VMEM((ROUNDS, 3, 48, 128), f32),
            pltpu.VMEM((2, ROUNDS, SENT, 128), f32),
            pltpu.VMEM((ROUNDS * SENT, 128), f32),
            pltpu.VMEM((ROUNDS * SENT, 128), f32),
            pltpu.VMEM((3, RP, 128), f32),
            pltpu.VMEM((CHUNKS, 128, 128), f32),
            pltpu.VMEM((BATCHES, 128, 128), f32),
            pltpu.VMEM((ROUNDS, CHUNKS, SLOTS, 128), f32),
            pltpu.VMEM((ROUNDS, CHUNKS, SLOTS, 128), f32),
            pltpu.VMEM((ACT, 128), f32),
            pltpu.VMEM((4, LP + RP, 128), f32),
            pltpu.VMEM((1 + BATCHES, 4, 128, 128), f32),
            pltpu.VMEM((1 + BATCHES, 3, 128, 128), f32),
            pltpu.VMEM((ROUNDS * SLOTS, RP), jnp.bfloat16),
            pltpu.VMEM((ACT, ROUNDS * SLOTS), jnp.bfloat16),
            pltpu.VMEM((LOW, 1, 128), f32),
            pltpu.VMEM((HIGH, 1, 128), f32),
            dma((2, ROUNDS)),
            dma((2, ROUNDS)),
            dma((len(PHASES), ROUNDS)),
            dma((len(PHASES), ROUNDS)),
            dma((LOW - 1,)),
            dma((LOW - 1,)),
            dma((HIGH - 1,)),
            dma((HIGH - 1,)),
        ],
        compiler_params=pltpu.CompilerParams(
            collective_id=0, has_side_effects=True, vmem_limit_bytes=63 * 1024 * 1024
        ),
    )(
        active_cells,
        active_counts,
        local_targets,
        local_sources,
        export_lists,
        remote_slots,
        remote_cells,
        local_targets.reshape(1, LP),
        remote_slots.reshape(RP // 128, 128),
        remote_cells.reshape(RP // 128, 128),
        velocities,
        particles,
    )


def solution(mesh):
    return jax.shard_map(
        shards,
        mesh=mesh,
        in_specs=(
            P(None, "dom", None),
            P(None, "dom", None),
            P("dom"),
            P("dom"),
            P("dom"),
            P("dom"),
            P("dom", None),
            P("dom"),
            P("dom"),
        ),
        out_specs=(P(None, "dom", None), P("dom", None)),
        check_vma=False,
    )
```
